32 devices in a mesh: groups: 2 (over x), node: 8 (over z, y), local: 2 (over core).
Axes of the slice: x: 2, y: 2, z: 4, core: 2. Of those that a mesh axis runs over, the one named last changes fastest.
Arguments:
- tokens: bfloat16 [2048, 3584], P(('groups', 'node'), 'local'), parts along dimension 0, may hold values from -6 to 6
- out_grad: bfloat16 [2048, 3584], P(('groups', 'node'), 'local'), parts along dimension 0, may hold values from -6 to 6
- route_weight: float32 [2048, 4], P(('groups', 'node')), parts along dimension 0, may hold values from 0.1 to 1
- expert_ids: int32 [2048, 4], P(('groups', 'node')), parts along dimension 0, may hold values from 0 to 7, all different within a row; in each aligned block of 128 rows (0 to 127, 128 to 255, ...) at most 96 rows name the same one
- w_gate: bfloat16 [8, 3584, 1024], P('node', None, 'local'), may hold values from -0.09375 to 0.09375
- w_up: bfloat16 [8, 3584, 1024], P('node', None, 'local'), may hold values from -0.09375 to 0.09375
- w_down: bfloat16 [8, 1024, 3584], P('node', 'local'), may hold values from -0.1875 to 0.1875
Outputs:
- in_grad: bfloat16 [2048, 3584], P(('groups', 'node'), 'local'), parts along dimension 0
The draws below stay inside these ranges and needn't reach their ends.
There are 2 independent parts, one for each index of `groups`. The reference program is written for one: setup_inputs(seed, part) draws one part's arguments, and reference() takes and returns one part's arrays. A program takes and returns all parts, laid end to end along the dimension named above; an argument that names none is the same for every part. Nothing has to cross between parts.
Inputs may be any that keep to these rules, and one draw needn't show every extreme that they name: `expert_ids`: A token names 4 different experts. Among the 128 tokens of one index of node no expert is named by more than 96 tokens, and in every draw some expert is named by exactly 96 of them.
All inputs are finite; a program needn't handle non-finite values.
Results may differ from the reference program's by a relative error of at most 0.0058.
Values may be sent and summed in bfloat16 or wider, within the bound.
No kernel may reach another device: no remote copies, remote signals or barrier semaphores. Data moves between devices by JAX's collectives and lax.ppermute only.
A program may use at most 128 MiB of HBM per device.

```python
import math
import jax
import jax.numpy as jnp
import numpy as np
from jax import lax

D = 3584
FF = 1024
TOP = 4
TOK_NODE = 128
EXPERTS = 8
CAP = 96
TOKENS = 1024
N_NODE = 8


def block_levels(key, shape, split, low, largest):
    factor_of = 1.0
    for axis_at, parts in split:
        draws = jax.random.uniform(jax.random.fold_in(jax.random.fold_in(key, 6), axis_at), (parts,), jnp.float32, low / len(split), largest / len(split))
        factor_of = factor_of * jnp.repeat(jnp.exp(draws), shape[axis_at] // parts).reshape((-1,) + (1,) * (len(shape) - 1 - axis_at))
    return factor_of


def shared_out(key, own, number, rows, number_of, top, limit, slope):
    ranking = jax.random.permutation(key, number_of)
    packed, common = portions_of(number_of, rows * top, limit, slope, True), portions_of(number_of, rows * top, limit, slope, False)
    places = jnp.arange(number_of)

    def named(lengths, rotation):
        used = int((lengths > 0).sum())
        fixed = max(1, used // 4)
        moved = fixed + (places - fixed + rotation * (used - fixed)) % max(1, number_of - fixed)
        return jnp.zeros((number_of,), jnp.int32).at[ranking[jnp.where(places < fixed, places, moved)]].set(jnp.asarray(lengths, jnp.int32))

    lengths = jnp.where(number % 4 == 0, named(packed, number // 4), named(common, number - number // 4 - 1))
    mixed = jax.random.permutation(jax.random.fold_in(own, 3), number_of)
    giver, sink = mixed[0:number_of // 2 * 2:2], mixed[1:number_of // 2 * 2:2]
    margin = jnp.minimum(lengths[giver] - 1, limit - lengths[sink]) // 2
    margin = jnp.where((giver == ranking[0]) | (sink == ranking[0]) | (lengths[sink] == 0), 0, jnp.maximum(margin, 0))
    moved = jax.random.randint(jax.random.fold_in(own, 4), (number_of // 2,), 0, 1 << 20) % (margin + 1)
    lengths = lengths.at[giver].add(-moved).at[sink].add(moved)
    labels = jnp.searchsorted(jnp.cumsum(lengths), jnp.arange(rows * top), side="right").astype(jnp.int32)
    table = labels.reshape(top, rows).T
    table = table[jax.random.permutation(jax.random.fold_in(own, 1), rows)]
    rotation = jax.random.randint(jax.random.fold_in(own, 2), (rows, 1), 0, top)
    return jnp.take_along_axis(table, (jnp.arange(top)[None, :] + rotation) % top, axis=1)


def portions_of(number_of, total, limit, lean, full):
    loads = [(1 << 20) // math.isqrt(standing ** lean) + 1 for standing in range(1, number_of + 1)]
    largest = limit if full else min(limit, max(-(-total // number_of), total * loads[0] // sum(loads)))
    least = 1 if total - largest >= number_of - 1 else 0
    given, surplus = [largest] + [least] * (number_of - 1), total - largest - least * (number_of - 1)
    while surplus > 0:
        movable = [i for i in range(1, number_of) if given[i] < largest] or [i for i in range(1, number_of) if given[i] < limit]
        mass, left = sum([loads[i] for i in movable]), surplus
        for i in movable:
            addition = min(limit - given[i], max(1, left * loads[i] // mass), surplus)
            given[i] = given[i] + addition
            surplus = surplus - addition
    return np.array(given)


def gaussian(key, shape, scale, most, shards=(), held_as=jnp.bfloat16):
    drawn = scale * jax.random.normal(key, shape, jnp.float32)
    if shards:
        drawn = drawn * block_levels(key, shape, shards, -0.22, 0.18)
    return jnp.clip(drawn, -most, most).astype(held_as)


def setup_inputs(seed: int = 0, part: int = 0) -> dict:
    keys = jax.random.split(jax.random.key(seed), 8)
    part_keys = jax.random.split(jax.random.fold_in(keys[7], part), 8)
    tokens = gaussian(part_keys[0], (TOKENS, D), 1.0, 6.0, ((0, 8), (1, 2)))
    out_grad = gaussian(part_keys[1], (TOKENS, D), 1.0, 6.0, ((0, 8), (1, 2)))
    route_weight = jnp.clip(0.1 + 0.9 * jax.random.uniform(part_keys[2], (TOKENS, TOP), jnp.float32) ** block_levels(part_keys[2], (TOKENS, TOP), ((0, 8),), -0.2, 0.2), 0.1, 1.0)
    expert_ids_keys = jax.random.split(jax.random.fold_in(part_keys[3], 1), TOKENS // TOK_NODE)
    expert_ids_turns = jax.random.permutation(jax.random.fold_in(part_keys[3], 3), TOKENS // TOK_NODE)
    expert_ids = jax.vmap(lambda own, number: shared_out(jax.random.fold_in(part_keys[3], 2), own, number, TOK_NODE, EXPERTS, TOP, CAP, 2))(expert_ids_keys, expert_ids_turns).reshape((TOKENS, TOP))
    w_gate = gaussian(keys[4], (EXPERTS, D, FF), D ** -0.5, 0.09375, ((0, 8), (2, 2)))
    w_up = gaussian(keys[5], (EXPERTS, D, FF), D ** -0.5, 0.09375, ((0, 8), (2, 2)))
    w_down = gaussian(keys[6], (EXPERTS, FF, D), FF ** -0.5, 0.1875, ((0, 8), (1, 2)))
    return {"tokens": tokens, "out_grad": out_grad, "route_weight": route_weight, "expert_ids": expert_ids, "w_gate": w_gate, "w_up": w_up, "w_down": w_down}


def expert_grad(feat_rows, cot_rows, gate_mat, up_mat, down_mat):
    numbers = (((1,), (1,)), ((), ()))
    gate_pre = jnp.dot(feat_rows, gate_mat, preferred_element_type=jnp.float32)
    up_pre = jnp.dot(feat_rows, up_mat, preferred_element_type=jnp.float32)
    hidden_grad = lax.dot_general(cot_rows, down_mat, numbers, preferred_element_type=jnp.float32)
    gate_sig = jax.nn.sigmoid(gate_pre)
    gate_grad = (hidden_grad * up_pre * gate_sig * (1.0 + gate_pre * (1.0 - gate_sig))).astype(jnp.bfloat16)
    up_grad = (hidden_grad * gate_pre * gate_sig).astype(jnp.bfloat16)
    summed = lax.dot_general(gate_grad, gate_mat, numbers, preferred_element_type=jnp.float32)
    return summed + lax.dot_general(up_grad, up_mat, numbers, preferred_element_type=jnp.float32)

def reference(tokens, out_grad, route_weight, expert_ids, w_gate, w_up, w_down):
    node_rows = TOK_NODE * TOP
    routed = TOKENS * TOP
    flat_ids = expert_ids.reshape(-1).astype(jnp.int32)
    onehot = (flat_ids.reshape(N_NODE, node_rows)[:, :, None] == jnp.arange(EXPERTS, dtype=jnp.int32)[None, None, :]).astype(jnp.int32)
    earlier = jnp.cumsum(onehot, axis=1) - onehot
    slot_index = lax.optimization_barrier(jnp.sum(earlier * onehot, axis=2)).reshape(-1)
    source = jnp.arange(routed, dtype=jnp.int32) // node_rows
    position = (flat_ids * N_NODE + source) * CAP + slot_index
    owners = jnp.full((EXPERTS * N_NODE * CAP,), routed, dtype=jnp.int32)
    owners = owners.at[position].set(jnp.arange(routed, dtype=jnp.int32))
    copies = jnp.concatenate([jnp.repeat(tokens, TOP, axis=0), jnp.zeros((1, D), tokens.dtype)], axis=0)
    scaled = (route_weight.reshape(-1)[:, None] * jnp.repeat(out_grad, TOP, axis=0).astype(jnp.float32)).astype(jnp.bfloat16)
    scaled = jnp.concatenate([scaled, jnp.zeros((1, D), scaled.dtype)], axis=0)

    def one_expert(pieces):
        expert_index, row_index = pieces
        result = expert_grad(copies[row_index], scaled[row_index], w_gate[expert_index], w_up[expert_index], w_down[expert_index])
        return result.astype(jnp.bfloat16)
    per_expert = lax.map(one_expert, (jnp.arange(EXPERTS, dtype=jnp.int32), owners.reshape(EXPERTS, N_NODE * CAP)))
    picked = per_expert.reshape(-1, D)[position]
    summed = out_grad.astype(jnp.float32) + lax.optimization_barrier(jnp.sum(picked.reshape(TOKENS, TOP, D).astype(jnp.float32), axis=1))
    return summed.astype(jnp.bfloat16)
```

```python
import jax
import jax.numpy as jnp
from jax import lax
from jax.sharding import PartitionSpec as P


def expert_grad(feat_rows, cot_rows, gate_mat, up_mat, down_mat):
    numbers = (((1,), (1,)), ((), ()))
    gate_pre = jnp.dot(feat_rows, gate_mat, preferred_element_type=jnp.float32)
    up_pre = jnp.dot(feat_rows, up_mat, preferred_element_type=jnp.float32)
    hidden_grad = lax.dot_general(cot_rows, down_mat, numbers, preferred_element_type=jnp.float32)
    gate_sig = jax.nn.sigmoid(gate_pre)
    gate_grad = (hidden_grad * up_pre * gate_sig * (1.0 + gate_pre * (1.0 - gate_sig))).astype(
        jnp.bfloat16
    )
    up_grad = (hidden_grad * gate_pre * gate_sig).astype(jnp.bfloat16)
    summed = lax.dot_general(gate_grad, gate_mat, numbers, preferred_element_type=jnp.float32)
    return summed + lax.dot_general(up_grad, up_mat, numbers, preferred_element_type=jnp.float32)


def exchanged(tokens, out_grad, route_weight, expert_ids, w_gate, w_up, w_down):
    tok_rows, half_width = tokens.shape
    top_count = expert_ids.shape[1]
    experts = lax.axis_size("node")
    capacity = 3 * tok_rows * top_count // (2 * experts)
    flat_ids = expert_ids.reshape(-1)
    onehot = (flat_ids[:, None] == jnp.arange(experts, dtype=jnp.int32)[None, :]).astype(jnp.int32)
    earlier = jnp.cumsum(onehot, axis=0) - onehot
    slot_index = jnp.sum(earlier * onehot, axis=1)
    target = flat_ids * capacity + slot_index
    scaled = (
        route_weight.reshape(-1)[:, None]
        * jnp.repeat(out_grad, top_count, axis=0).astype(jnp.float32)
    ).astype(jnp.bfloat16)
    copies = jnp.repeat(tokens, top_count, axis=0)
    feat_send = jnp.zeros((experts * capacity, half_width), jnp.bfloat16).at[target].set(copies)
    cot_send = jnp.zeros((experts * capacity, half_width), jnp.bfloat16).at[target].set(scaled)
    feat_send = feat_send.reshape(experts, capacity, half_width)
    cot_send = cot_send.reshape(experts, capacity, half_width)

    def to_experts(sent):
        moved = lax.all_to_all(sent, "node", split_axis=0, concat_axis=0, tiled=True)
        return lax.all_gather(moved, "local", axis=2, tiled=True)

    feat_full = to_experts(feat_send)
    cot_full = to_experts(cot_send)
    sources, slot_count, feat_width = feat_full.shape
    partial_value = expert_grad(
        feat_full.reshape(-1, feat_width),
        cot_full.reshape(-1, feat_width),
        w_gate[0],
        w_up[0],
        w_down[0],
    )
    own_sum = lax.psum_scatter(
        partial_value.reshape(sources, slot_count, feat_width),
        "local",
        scatter_dimension=2,
        tiled=True,
    )
    returned = lax.all_to_all(
        own_sum.astype(jnp.bfloat16), "node", split_axis=0, concat_axis=0, tiled=True
    )
    picked = returned.reshape(experts * capacity, half_width)[target]
    summed = out_grad.astype(jnp.float32) + jnp.sum(
        picked.reshape(tok_rows, top_count, half_width).astype(jnp.float32), axis=1
    )
    return summed.astype(jnp.bfloat16)


def node(z, y):
    return 2 * z + y


def along(pairs):
    return [(node(a, y), node(b, y)) for a, b in pairs for y in range(2)]


def across(places):
    return [(node(z, y), node(z, 1 - y)) for z in places for y in range(2)]


UP1 = along([(0, 1), (1, 2), (2, 3)])
DOWN1 = along([(1, 0), (2, 1), (3, 2)])
UP2 = along([(1, 2), (2, 3)])
DOWN2 = along([(2, 1), (1, 0)])
ENDS = along([(2, 3), (1, 0)])
SKIP = along([(0, 2), (1, 3), (2, 0), (3, 1)])
FAR = along([(0, 3), (3, 0)])
Y_ALL, Y_UP, Y_DOWN, Y_ENDS = across(range(4)), across([1, 2, 3]), across([0, 1, 2]), across([0, 3])


def move(value, pairs):
    return lax.ppermute(value, "node", pairs)


def swap(value):
    return lax.ppermute(value, "local", [(0, 1), (1, 0)])


def one_hot_slots(weights, capacity):
    tokens = weights.shape[-1]
    routed = weights > 0.0
    earlier = jnp.arange(tokens)[:, None] < jnp.arange(tokens)[None, :]
    place = jnp.einsum(
        "...s,st->...t",
        routed.astype(jnp.bfloat16),
        earlier.astype(jnp.bfloat16),
        preferred_element_type=jnp.float32,
    )
    place = jnp.where(routed, place, -1.0)
    slots = jnp.arange(capacity, dtype=jnp.float32)
    return (place[..., None, :] == slots[:, None]).astype(jnp.bfloat16)


def lines(tokens, out_grad, route_weight, expert_ids, w_gate, w_up, w_down):
    tok_rows, half = tokens.shape
    experts = lax.axis_size("node")
    top_count = expert_ids.shape[1]
    capacity = 3 * tok_rows * top_count // (2 * experts)
    me = lax.axis_index("node")
    z, y = me // 2, me % 2
    side = lax.axis_index("local")
    bf, f32 = jnp.bfloat16, jnp.float32

    t_up, t_down = move(tokens, UP1), move(tokens, DOWN1)
    g_up, g_down = move(out_grad, UP1), move(out_grad, DOWN1)

    table = jnp.sum(
        jnp.where(
            expert_ids[None] == jnp.arange(experts, dtype=jnp.int32)[:, None, None],
            route_weight[None],
            0.0,
        ),
        axis=2,
    )
    pairs = table.reshape(experts // 2, 1, 2, tok_rows)
    routes = lax.all_to_all(
        jnp.broadcast_to(pairs, (experts // 2, 2, 2, tok_rows)).reshape(experts, 2, tok_rows),
        "node",
        split_axis=0,
        concat_axis=0,
        tiled=True,
    )
    own_pick = one_hot_slots(lax.dynamic_index_in_dim(table, me ^ 1, 0, False), capacity)
    places = jnp.stack([z, z - 1, z + 1, z ^ 2, 3 - z]) % 4
    mine = routes[places * 2 + y]
    theirs = routes[places * 2 + 1 - y]
    dense_weight = jnp.take(mine, y, axis=1)
    picks = one_hot_slots(jnp.take(mine, 1 - y, axis=1), capacity)
    slot_weights = jnp.take(theirs, y, axis=1)
    slot_picks = one_hot_slots(slot_weights, capacity)
    slot_weight = jnp.sum(slot_picks.astype(f32) * slot_weights[:, None, :], axis=2)

    gate, up, down = w_gate[0], w_up[0], w_down[0]
    own_at, other_at = side * half, (1 - side) * half
    rows = lambda mat, at: lax.dynamic_slice_in_dim(mat, at, half, 0)
    cols = lambda mat, at: lax.dynamic_slice_in_dim(mat, at, half, 1)
    both = [jnp.concatenate([rows(gate, at), rows(up, at)], axis=1) for at in (own_at, other_at)]
    back = jnp.concatenate([both[0], swap(both[1])], axis=1)
    downs = [cols(down, own_at), cols(down, other_at)]
    numbers = (((1,), (1,)), ((), ()))
    ff = gate.shape[1]

    def dot(a, b):
        return jnp.dot(a, b, preferred_element_type=f32)

    def dot_t(a, b):
        return lax.dot_general(a, b, numbers, preferred_element_type=f32)

    def compute(feat, cot, weight):
        feat, cot = jnp.concatenate(feat, 0), jnp.concatenate(cot, 0)
        feat_other, cot_other = swap(feat), swap(cot)
        pre = dot(feat, both[0]) + dot(feat_other, both[1])
        hidden = (dot_t(cot, downs[0]) + dot_t(cot_other, downs[1])) * weight[:, None]
        gate_pre, up_pre = pre[:, :ff], pre[:, ff:]
        sig = jax.nn.sigmoid(gate_pre)
        gate_grad = (hidden * up_pre * sig * (1.0 + gate_pre * (1.0 - sig))).astype(bf)
        up_grad = (hidden * gate_pre * sig).astype(bf)
        grads = jnp.concatenate([gate_grad, up_grad], axis=1)
        grads = jnp.concatenate([grads, swap(grads)], axis=1)
        return dot_t(grads, back)

    def across_rows(index, block, pairs, pick=None):
        pick = picks[index] if pick is None else pick
        return move(dot(pick, block).astype(bf), pairs)

    def finish(index, dense, slots, pairs, pick=None):
        pick = picks[index] if pick is None else pick
        came = move(slots.astype(bf), pairs)
        return dense + lax.dot_general(
            pick, came, (((0,), (0,)), ((), ())), preferred_element_type=f32
        )

    t_own_y = across_rows(0, tokens, Y_ALL, own_pick)
    g_own_y = across_rows(0, out_grad, Y_ALL, own_pick)
    t2u, t2d = move(t_up, UP2), move(t_down, DOWN2)
    t_up_y, t_down_y = across_rows(1, t_up, Y_UP), across_rows(2, t_down, Y_DOWN)
    g2u, g2d = move(g_up, UP2), move(g_down, DOWN2)
    g_up_y, g_down_y = across_rows(1, g_up, Y_UP), across_rows(2, g_down, Y_DOWN)
    t_two = jnp.where(z >= 2, t2u, t2d)
    g_two = jnp.where(z >= 2, g2u, g2d)
    t_far = move(t_two, ENDS)
    t_two_y = across_rows(3, t_two, Y_ALL)
    g_far = move(g_two, ENDS)
    g_two_y = across_rows(3, g_two, Y_ALL)
    t_far_y = across_rows(4, t_far, Y_ENDS)
    g_far_y = across_rows(4, g_far, Y_ENDS)

    n, c = tok_rows, capacity
    first = compute(
        [tokens, t_up, t_down, t_own_y, t_up_y, t_down_y],
        [out_grad, g_up, g_down, g_own_y, g_up_y, g_down_y],
        jnp.concatenate([dense_weight[:3].reshape(-1), slot_weight[:3].reshape(-1)]),
    )
    s = 3 * n
    own = finish(0, first[:n], first[s : s + c], Y_ALL, own_pick)
    from_up = move(finish(1, first[n : 2 * n], first[s + c : s + 2 * c], Y_UP).astype(bf), DOWN1)
    from_down = move(
        finish(2, first[2 * n : s], first[s + 2 * c :], Y_DOWN).astype(bf), UP1
    )
    second = compute(
        [t_two, t_two_y], [g_two, g_two_y], jnp.concatenate([dense_weight[3], slot_weight[3]])
    )
    from_two = move(finish(3, second[:n], second[n:], Y_ALL).astype(bf), SKIP)
    third = compute(
        [t_far, t_far_y], [g_far, g_far_y], jnp.concatenate([dense_weight[4], slot_weight[4]])
    )
    from_far = move(finish(4, third[:n], third[n:], Y_ENDS).astype(bf), FAR)
    summed = out_grad.astype(f32) + own
    for part in (from_up, from_down, from_two, from_far):
        summed = summed + part.astype(f32)
    return summed.astype(bf)


def solution(mesh):
    placed = (
        P(("groups", "node"), "local"),
        P(("groups", "node"), "local"),
        P(("groups", "node"), None),
        P(("groups", "node"), None),
        P("node", None, "local"),
        P("node", None, "local"),
        P("node", "local", None),
    )
    body = lines if mesh.shape["node"] == 8 else exchanged
    return jax.shard_map(
        body, mesh=mesh, in_specs=placed, out_specs=P(("groups", "node"), "local"), check_vma=False
    )
```

```python
import functools

import jax
import jax.numpy as jnp
from jax import lax
from jax.experimental import pallas as pl
from jax.experimental.pallas import tpu as pltpu
from jax.sharding import PartitionSpec as P


def expert_grad(feat_rows, cot_rows, gate_mat, up_mat, down_mat):
    numbers = (((1,), (1,)), ((), ()))
    gate_pre = jnp.dot(feat_rows, gate_mat, preferred_element_type=jnp.float32)
    up_pre = jnp.dot(feat_rows, up_mat, preferred_element_type=jnp.float32)
    hidden_grad = lax.dot_general(cot_rows, down_mat, numbers, preferred_element_type=jnp.float32)
    gate_sig = jax.nn.sigmoid(gate_pre)
    gate_grad = (hidden_grad * up_pre * gate_sig * (1.0 + gate_pre * (1.0 - gate_sig))).astype(
        jnp.bfloat16
    )
    up_grad = (hidden_grad * gate_pre * gate_sig).astype(jnp.bfloat16)
    summed = lax.dot_general(gate_grad, gate_mat, numbers, preferred_element_type=jnp.float32)
    return summed + lax.dot_general(up_grad, up_mat, numbers, preferred_element_type=jnp.float32)


def exchanged(tokens, out_grad, route_weight, expert_ids, w_gate, w_up, w_down):
    tok_rows, half_width = tokens.shape
    top_count = expert_ids.shape[1]
    experts = lax.axis_size("node")
    capacity = 3 * tok_rows * top_count // (2 * experts)
    flat_ids = expert_ids.reshape(-1)
    onehot = (flat_ids[:, None] == jnp.arange(experts, dtype=jnp.int32)[None, :]).astype(jnp.int32)
    earlier = jnp.cumsum(onehot, axis=0) - onehot
    slot_index = jnp.sum(earlier * onehot, axis=1)
    target = flat_ids * capacity + slot_index
    scaled = (
        route_weight.reshape(-1)[:, None]
        * jnp.repeat(out_grad, top_count, axis=0).astype(jnp.float32)
    ).astype(jnp.bfloat16)
    copies = jnp.repeat(tokens, top_count, axis=0)
    feat_send = jnp.zeros((experts * capacity, half_width), jnp.bfloat16).at[target].set(copies)
    cot_send = jnp.zeros((experts * capacity, half_width), jnp.bfloat16).at[target].set(scaled)
    feat_send = feat_send.reshape(experts, capacity, half_width)
    cot_send = cot_send.reshape(experts, capacity, half_width)

    def to_experts(sent):
        moved = lax.all_to_all(sent, "node", split_axis=0, concat_axis=0, tiled=True)
        return lax.all_gather(moved, "local", axis=2, tiled=True)

    feat_full = to_experts(feat_send)
    cot_full = to_experts(cot_send)
    sources, slot_count, feat_width = feat_full.shape
    partial_value = expert_grad(
        feat_full.reshape(-1, feat_width),
        cot_full.reshape(-1, feat_width),
        w_gate[0],
        w_up[0],
        w_down[0],
    )
    own_sum = lax.psum_scatter(
        partial_value.reshape(sources, slot_count, feat_width),
        "local",
        scatter_dimension=2,
        tiled=True,
    )
    returned = lax.all_to_all(
        own_sum.astype(jnp.bfloat16), "node", split_axis=0, concat_axis=0, tiled=True
    )
    picked = returned.reshape(experts * capacity, half_width)[target]
    summed = out_grad.astype(jnp.float32) + jnp.sum(
        picked.reshape(tok_rows, top_count, half_width).astype(jnp.float32), axis=1
    )
    return summed.astype(jnp.bfloat16)


def node(z, y):
    return 2 * z + y


def along(pairs):
    return [(node(a, y), node(b, y)) for a, b in pairs for y in range(2)]


def across(places):
    return [(node(z, y), node(z, 1 - y)) for z in places for y in range(2)]


UP1 = along([(0, 1), (1, 2), (2, 3)])
DOWN1 = along([(1, 0), (2, 1), (3, 2)])
UP2 = along([(1, 2), (2, 3)])
DOWN2 = along([(2, 1), (1, 0)])
ENDS = along([(2, 3), (1, 0)])
SKIP = along([(0, 2), (1, 3), (2, 0), (3, 1)])
FAR = along([(0, 3), (3, 0)])
Y_ALL, Y_UP, Y_DOWN, Y_ENDS = across(range(4)), across([1, 2, 3]), across([0, 1, 2]), across([0, 3])
SLOTS = 5
BF, F32 = jnp.bfloat16, jnp.float32
ON_CHIP = pl.BlockSpec(memory_space=pltpu.VMEM)
ON_CHIP_SCALARS = pl.BlockSpec(memory_space=pltpu.SMEM)
ANYWHERE = pl.BlockSpec(memory_space=pl.ANY)
SMALL = pl.CostEstimate(flops=1024, bytes_accessed=1024, transcendentals=0)


def move(value, pairs):
    return lax.ppermute(value, "node", pairs)


def swap(value):
    return lax.ppermute(value, "local", [(0, 1), (1, 0)])


def dot(a, b):
    return jnp.dot(a, b, preferred_element_type=F32)


def dot_t(a, b):
    return lax.dot_general(a, b, (((1,), (1,)), ((), ())), preferred_element_type=F32)


def params():
    return pltpu.CompilerParams(vmem_limit_bytes=16 * 1024 * 1024)


def places_of(weights):
    tokens = weights.shape[-1]
    earlier = lax.broadcasted_iota(jnp.int32, (tokens, tokens), 0) < lax.broadcasted_iota(
        jnp.int32, (tokens, tokens), 1
    )
    routed = (weights > 0.0).astype(F32)
    place = dot(routed.astype(BF), earlier.astype(F32).astype(BF))
    return jnp.where(weights > 0.0, place, -1.0)


def pick_of(place, capacity):
    slots = lax.broadcasted_iota(jnp.int32, (capacity, place.shape[-1]), 0).astype(F32)
    return jnp.where(slots == place, 1.0, 0.0).astype(F32)


def routes_kernel(capacity, at, routes, place_out, weight_out):
    z, y = at[0], at[1]
    first = y == 0
    tokens = routes.shape[-1]
    sent, dense, slots = [], [], []
    for where in (z, z + 3, z + 1, z ^ 2, 3 - z):
        where = lax.rem(where, 4)
        mine, theirs = routes[2 * where + y], routes[2 * where + 1 - y]
        dense.append(jnp.where(first, mine[0:1], mine[1:2]))
        sent.append(jnp.where(first, mine[1:2], mine[0:1]))
        slots.append(jnp.where(first, theirs[0:1], theirs[1:2]))
    pad = [jnp.zeros((16 - 2 * SLOTS, tokens), F32)]
    place = places_of(jnp.concatenate(sent + slots + pad, axis=0))
    same = lax.broadcasted_iota(jnp.int32, (tokens, tokens), 0) == lax.broadcasted_iota(
        jnp.int32, (tokens, tokens), 1
    )
    for i in range(SLOTS):
        place_out[i] = place[i : i + 1]
        weight_out[i, :tokens] = jnp.sum(jnp.where(same, dense[i], 0.0), axis=1, keepdims=True)
        pick = pick_of(place[SLOTS + i : SLOTS + i + 1], capacity)
        weight_out[i, tokens:] = jnp.sum(pick * slots[i], axis=1, keepdims=True)


def route_tables(at, routes, capacity):
    tokens = routes.shape[-1]
    return pl.pallas_call(
        functools.partial(routes_kernel, capacity),
        out_shape=[
            jax.ShapeDtypeStruct((SLOTS, 1, tokens), F32),
            jax.ShapeDtypeStruct((SLOTS, tokens + capacity, 1), F32),
        ],
        in_specs=[pl.BlockSpec(memory_space=pltpu.SMEM), pl.BlockSpec(memory_space=pltpu.VMEM)],
        out_specs=[pl.BlockSpec(memory_space=pltpu.VMEM)] * 2,
        compiler_params=params(),
        cost_estimate=SMALL,
        name="routes",
    )(at, routes)


def pick_kernel(capacity, place, both, *rest):
    out = rest[-1]
    tokens = place.shape[-1]
    pick = pick_of(place[...], capacity).astype(BF)
    out[:capacity] = dot(pick, both[:tokens]).astype(BF)
    out[capacity:] = dot(pick, both[tokens:]).astype(BF)


def picked_rows(place, both, capacity, after=()):
    return pl.pallas_call(
        functools.partial(pick_kernel, capacity),
        out_shape=jax.ShapeDtypeStruct((2 * capacity, both.shape[1]), BF),
        in_specs=[pl.BlockSpec(memory_space=pltpu.VMEM)] * 2 + [ANYWHERE] * len(after),
        out_specs=pl.BlockSpec(memory_space=pltpu.VMEM),
        compiler_params=params(),
        cost_estimate=SMALL,
        name="pick",
    )(place, both, *after)


def grads_kernel(side, block, block_far, slots, slots_far, weight, gate, up, down, *rest):
    out = rest[-1]
    capacity, tokens, half = slots.shape[0] // 2, block.shape[0] // 2, block.shape[1]
    ff = gate.shape[1]
    near = pl.ds(pl.multiple_of(side[0] * half, 256), half)
    far = pl.ds(pl.multiple_of((1 - side[0]) * half, 256), half)

    def feats(block, slots):
        return jnp.concatenate([block[:tokens], slots[:capacity]], axis=0)

    def cots(block, slots):
        return jnp.concatenate([block[tokens:], slots[capacity:]], axis=0)

    width = ff // 2
    for at in range(0, ff, width):
        cols = slice(at, at + width)
        rows, rows_far = feats(block, slots), feats(block_far, slots_far)
        gate_pre = dot(rows, gate[near, cols]) + dot(rows_far, gate[far, cols])
        up_pre = dot(rows, up[near, cols]) + dot(rows_far, up[far, cols])
        rows, rows_far = cots(block, slots), cots(block_far, slots_far)
        hidden = dot_t(rows, down[cols, near]) + dot_t(rows_far, down[cols, far])
        hidden = hidden * weight[...]
        sig = jax.nn.sigmoid(gate_pre)
        out[:, cols] = (hidden * up_pre * sig * (1.0 + gate_pre * (1.0 - sig))).astype(BF)
        out[:, ff + at : ff + at + width] = (hidden * gate_pre * sig).astype(BF)


def grads_of(side, block, slots, weight, mats, after=()):
    rows = (block[0].shape[0] + slots[0].shape[0]) // 2
    return pl.pallas_call(
        grads_kernel,
        out_shape=jax.ShapeDtypeStruct((rows, 2 * mats[0].shape[1]), BF),
        in_specs=[ON_CHIP_SCALARS] + [ON_CHIP] * 8 + [ANYWHERE] * len(after),
        out_specs=ON_CHIP,
        compiler_params=params(),
        cost_estimate=SMALL,
        name="grads",
    )(side, *block, *slots, weight, *mats, *after)


def back_kernel(side, own, other, gate, up, far, *rest):
    dense, slots = rest[-2:]
    tokens, half = dense.shape
    ff = gate.shape[1]
    width = 256
    for at in range(0, half, width):
        near, cols = pl.ds(pl.multiple_of(side[0] * half + at, 256), width), slice(at, at + width)
        total = dot_t(own[:, :ff], gate[near, :]) + dot_t(own[:, ff:], up[near, :])
        total += dot_t(other[:, :ff], far[0, cols]) + dot_t(other[:, ff:], far[1, cols])
        dense[:, cols] = total[:tokens]
        slots[:, cols] = total[tokens:].astype(BF)


def back_of(side, own, other, mats, mats_far, tokens, after=()):
    rows, half = own.shape[0], mats_far.shape[1]
    return pl.pallas_call(
        back_kernel,
        out_shape=[
            jax.ShapeDtypeStruct((tokens, half), F32),
            jax.ShapeDtypeStruct((rows - tokens, half), BF),
        ],
        in_specs=[ON_CHIP_SCALARS] + [ON_CHIP] * 5 + [ANYWHERE] * len(after),
        out_specs=[ON_CHIP] * 2,
        compiler_params=params(),
        cost_estimate=SMALL,
        name="back",
    )(side, own, other, *mats, mats_far, *after)


def spread(place, came):
    pick = pick_of(place, came.shape[0]).astype(BF)
    return lax.dot_general(pick, came, (((0,), (0,)), ((), ())), preferred_element_type=F32)


def join_kernel(parts, place, came, dense, *rest):
    out = rest[-1]
    total = dense[...] + spread(place[...], came[...])
    for part in rest[:parts]:
        total = total + part[...].astype(F32)
    out[...] = total.astype(out.dtype)


def joined(place, came, dense, parts=(), dtype=BF, after=()):
    return pl.pallas_call(
        functools.partial(join_kernel, len(parts)),
        out_shape=jax.ShapeDtypeStruct(dense.shape, dtype),
        in_specs=[pl.BlockSpec(memory_space=pltpu.VMEM)] * (3 + len(parts))
        + [ANYWHERE] * len(after),
        out_specs=pl.BlockSpec(memory_space=pltpu.VMEM),
        compiler_params=params(),
        cost_estimate=SMALL,
        name="join",
    )(place, came, dense, *parts, *after)


def lines(tokens, out_grad, route_weight, expert_ids, w_gate, w_up, w_down):
    tok_rows, half = tokens.shape
    experts = lax.axis_size("node")
    top_count = expert_ids.shape[1]
    capacity = 3 * tok_rows * top_count // (2 * experts)
    me = lax.axis_index("node")
    z, y = me // 2, me % 2
    at = jnp.stack([z, y]).astype(jnp.int32)
    side = lax.axis_index("local").astype(jnp.int32)
    side1 = side[None]

    both = jnp.concatenate([tokens, out_grad], axis=0)
    b_up, b_down = move(both, UP1), move(both, DOWN1)

    table = jnp.sum(
        jnp.where(
            expert_ids[None] == jnp.arange(experts, dtype=jnp.int32)[:, None, None],
            route_weight[None],
            0.0,
        ),
        axis=2,
    )
    own_place = places_of(lax.dynamic_slice_in_dim(table, me ^ 1, 1, 0))
    own_rows = picked_rows(own_place, both, capacity)
    pairs = table.reshape(experts // 2, 1, 2, tok_rows)
    routes = lax.all_to_all(
        jnp.broadcast_to(pairs, (experts // 2, 2, 2, tok_rows)).reshape(experts, 2, tok_rows),
        "node",
        split_axis=0,
        concat_axis=0,
        tiled=True,
    )
    places, weights = route_tables(at, routes, capacity)

    gate, up, down = w_gate[0], w_up[0], w_down[0]
    gate_late, up_late, own_rows = lax.optimization_barrier((gate, up, own_rows))
    other = lambda mat: lax.dynamic_slice_in_dim(mat, (1 - side) * half, half, 0)
    far_mats = swap(jnp.stack([other(gate_late), other(up_late)]))

    def halves(block):
        return block, swap(block)

    def late(value, *before):
        return lax.optimization_barrier((value, *before))[0]

    def back(own, other, after=()):
        return back_of(side1, own, other, (gate, up), far_mats, tok_rows, after)

    def grads(index, block, slots, after=()):
        return grads_of(side1, block, slots, weights[index], (gate, up, down), after)

    own_y = move(own_rows, Y_ALL)
    own_halves, own_slots = halves(both), halves(own_y)

    b_up, b_down, places, *_ = lax.optimization_barrier(
        (b_up, b_down, places, far_mats, own_halves, own_slots)
    )
    up_two, down_two = move(b_up, UP2), move(b_down, DOWN2)
    up_rows = picked_rows(places[1], b_up, capacity)
    up_y = move(up_rows, Y_UP)
    down_rows = picked_rows(places[2], b_down, capacity, (up_rows,))
    down_y = move(down_rows, Y_DOWN)
    grads0 = grads(0, own_halves, own_slots, (down_rows,))

    up_two, down_two, grads0, up_y = lax.optimization_barrier((up_two, down_two, grads0, up_y))
    b_two = jnp.where(z >= 2, up_two, down_two)
    b_far = move(b_two, ENDS)
    two_rows = picked_rows(places[3], b_two, capacity)
    two_y = move(two_rows, Y_ALL)
    dense0, slots0 = back(grads0, swap(grads0), (two_rows,))
    grads1 = grads(1, halves(late(b_up, up_two)), halves(up_y), (dense0,))
    grads2 = grads(2, halves(late(b_down, up_two)), halves(down_y), (grads1,))

    b_far, grads1, grads2, slots0, two_y = lax.optimization_barrier(
        (b_far, grads1, grads2, slots0, two_y)
    )
    far_rows = picked_rows(places[4], b_far, capacity)
    far_y = move(far_rows, Y_ENDS)
    dense1, slots1 = back(grads1, swap(grads1), (far_rows,))
    came1 = move(slots1, Y_UP)
    dense2, slots2 = back(grads2, swap(grads2), (dense1,))
    grads3 = grads(3, halves(b_two), halves(two_y), (dense2,))
    far_halves = halves(b_far)

    far_y, grads3, came1, far_halves, dense2, slots2 = lax.optimization_barrier(
        (far_y, grads3, came1, far_halves, dense2, slots2)
    )
    came2 = move(slots2, Y_DOWN)
    home1 = move(joined(places[1], came1, dense1), DOWN1)
    dense3, slots3 = back(grads3, swap(grads3))
    grads4 = grads(4, far_halves, halves(far_y), (dense3,))
    came2, slots3, grads4 = lax.optimization_barrier((came2, slots3, grads4))
    came3 = move(slots3, Y_ALL)
    home2 = move(joined(places[2], came2, dense2), UP1)
    dense4, slots4 = back(grads4, swap(grads4))
    came4 = move(slots4, Y_ENDS)
    home3 = move(joined(places[3], came3, dense3), SKIP)
    came0 = move(late(slots0, dense4), Y_ALL)
    own = joined(own_place, came0, dense0, (out_grad,), F32)
    summed = own + home1.astype(F32)
    home4 = move(joined(places[4], came4, dense4), FAR)
    for value in (home2, home3, home4):
        summed = summed + value.astype(F32)
    return summed.astype(BF)


def solution(mesh):
    placed = (
        P(("groups", "node"), "local"),
        P(("groups", "node"), "local"),
        P(("groups", "node"), None),
        P(("groups", "node"), None),
        P("node", None, "local"),
        P("node", None, "local"),
        P("node", "local", None),
    )
    body = lines if mesh.shape["node"] == 8 else exchanged
    return jax.shard_map(
        body, mesh=mesh, in_specs=placed, out_specs=P(("groups", "node"), "local"), check_vma=False
    )
```

```python
import functools

import jax
import jax.numpy as jnp
from jax import lax
from jax.experimental import pallas as pl
from jax.experimental.pallas import tpu as pltpu
from jax.sharding import PartitionSpec as P


def expert_grad(feat_rows, cot_rows, gate_mat, up_mat, down_mat):
    numbers = (((1,), (1,)), ((), ()))
    gate_pre = jnp.dot(feat_rows, gate_mat, preferred_element_type=jnp.float32)
    up_pre = jnp.dot(feat_rows, up_mat, preferred_element_type=jnp.float32)
    hidden_grad = lax.dot_general(cot_rows, down_mat, numbers, preferred_element_type=jnp.float32)
    gate_sig = jax.nn.sigmoid(gate_pre)
    gate_grad = (hidden_grad * up_pre * gate_sig * (1.0 + gate_pre * (1.0 - gate_sig))).astype(
        jnp.bfloat16
    )
    up_grad = (hidden_grad * gate_pre * gate_sig).astype(jnp.bfloat16)
    summed = lax.dot_general(gate_grad, gate_mat, numbers, preferred_element_type=jnp.float32)
    return summed + lax.dot_general(up_grad, up_mat, numbers, preferred_element_type=jnp.float32)


def exchanged(tokens, out_grad, route_weight, expert_ids, w_gate, w_up, w_down):
    tok_rows, half_width = tokens.shape
    top_count = expert_ids.shape[1]
    experts = lax.axis_size("node")
    capacity = 3 * tok_rows * top_count // (2 * experts)
    flat_ids = expert_ids.reshape(-1)
    onehot = (flat_ids[:, None] == jnp.arange(experts, dtype=jnp.int32)[None, :]).astype(jnp.int32)
    earlier = jnp.cumsum(onehot, axis=0) - onehot
    slot_index = jnp.sum(earlier * onehot, axis=1)
    target = flat_ids * capacity + slot_index
    scaled = (
        route_weight.reshape(-1)[:, None]
        * jnp.repeat(out_grad, top_count, axis=0).astype(jnp.float32)
    ).astype(jnp.bfloat16)
    copies = jnp.repeat(tokens, top_count, axis=0)
    feat_send = jnp.zeros((experts * capacity, half_width), jnp.bfloat16).at[target].set(copies)
    cot_send = jnp.zeros((experts * capacity, half_width), jnp.bfloat16).at[target].set(scaled)
    feat_send = feat_send.reshape(experts, capacity, half_width)
    cot_send = cot_send.reshape(experts, capacity, half_width)

    def to_experts(sent):
        moved = lax.all_to_all(sent, "node", split_axis=0, concat_axis=0, tiled=True)
        return lax.all_gather(moved, "local", axis=2, tiled=True)

    feat_full = to_experts(feat_send)
    cot_full = to_experts(cot_send)
    sources, slot_count, feat_width = feat_full.shape
    partial_value = expert_grad(
        feat_full.reshape(-1, feat_width),
        cot_full.reshape(-1, feat_width),
        w_gate[0],
        w_up[0],
        w_down[0],
    )
    own_sum = lax.psum_scatter(
        partial_value.reshape(sources, slot_count, feat_width),
        "local",
        scatter_dimension=2,
        tiled=True,
    )
    returned = lax.all_to_all(
        own_sum.astype(jnp.bfloat16), "node", split_axis=0, concat_axis=0, tiled=True
    )
    picked = returned.reshape(experts * capacity, half_width)[target]
    summed = out_grad.astype(jnp.float32) + jnp.sum(
        picked.reshape(tok_rows, top_count, half_width).astype(jnp.float32), axis=1
    )
    return summed.astype(jnp.bfloat16)


def node(z, y):
    return 2 * z + y


def along(pairs):
    return [(node(a, y), node(b, y)) for a, b in pairs for y in range(2)]


def across(places):
    return [(node(z, y), node(z, 1 - y)) for z in places for y in range(2)]


UP1 = along([(0, 1), (1, 2), (2, 3)])
DOWN1 = along([(1, 0), (2, 1), (3, 2)])
UP2 = along([(1, 2), (2, 3)])
DOWN2 = along([(2, 1), (1, 0)])
ENDS = along([(2, 3), (1, 0)])
SKIP = along([(0, 2), (1, 3), (2, 0), (3, 1)])
FAR = along([(0, 3), (3, 0)])
Y_ALL, Y_UP, Y_DOWN, Y_ENDS = across(range(4)), across([1, 2, 3]), across([0, 1, 2]), across([0, 3])
SLOTS = 5
BF, F32 = jnp.bfloat16, jnp.float32
ON_CHIP = pl.BlockSpec(memory_space=pltpu.VMEM)
ON_CHIP_SCALARS = pl.BlockSpec(memory_space=pltpu.SMEM)
ANYWHERE = pl.BlockSpec(memory_space=pl.ANY)
SMALL = pl.CostEstimate(flops=1024, bytes_accessed=1024, transcendentals=0)


def move(value, pairs):
    return lax.ppermute(value, "node", pairs)


def swap(value):
    return lax.ppermute(value, "local", [(0, 1), (1, 0)])


def dot(a, b):
    return jnp.dot(a, b, preferred_element_type=F32)


def dot_t(a, b):
    return lax.dot_general(a, b, (((1,), (1,)), ((), ())), preferred_element_type=F32)


def params():
    return pltpu.CompilerParams(vmem_limit_bytes=16 * 1024 * 1024)


def places_of(weights):
    tokens = weights.shape[-1]
    earlier = lax.broadcasted_iota(jnp.int32, (tokens, tokens), 0) < lax.broadcasted_iota(
        jnp.int32, (tokens, tokens), 1
    )
    routed = (weights > 0.0).astype(F32)
    place = dot(routed.astype(BF), earlier.astype(F32).astype(BF))
    return jnp.where(weights > 0.0, place, -1.0)


def pick_of(place, capacity):
    slots = lax.broadcasted_iota(jnp.int32, (capacity, place.shape[-1]), 0).astype(F32)
    return jnp.where(slots == place, 1.0, 0.0).astype(F32)


def stack_kernel(feat, cot, table, out):
    tokens, half = feat.shape
    out[:tokens] = feat[...]
    out[tokens : 2 * tokens] = cot[...]
    value = table[...]
    high = value.astype(BF).astype(F32)
    middle = (value - high).astype(BF).astype(F32)
    low = value - high - middle
    upper = jnp.concatenate([high, low], axis=1)
    lower = jnp.concatenate([middle, jnp.zeros_like(low)], axis=1)
    rows = jnp.concatenate([upper, lower], axis=0)
    rest = jnp.zeros((rows.shape[0], half - rows.shape[1]), F32)
    out[2 * tokens :] = jnp.concatenate([rows, rest], axis=1).astype(BF)


def stacked(feat, cot, table):
    tokens, half = feat.shape
    return pl.pallas_call(
        stack_kernel,
        out_shape=jax.ShapeDtypeStruct((2 * tokens + 2 * table.shape[0], half), BF),
        in_specs=[ON_CHIP] * 3,
        out_specs=ON_CHIP,
        compiler_params=params(),
        cost_estimate=SMALL,
        name="stack",
    )(feat, cot, table)


def route_row(ref, first, height, tokens, expert):
    rows = ref[first : first + height, : 2 * tokens].astype(F32)
    count = rows.shape[0] // 2
    table = rows[:count, :tokens] + rows[count:, :tokens] + rows[:count, tokens:]
    chosen = lax.broadcasted_iota(jnp.int32, table.shape, 0) == expert
    return jnp.sum(jnp.where(chosen, table, 0.0), axis=0, keepdims=True)


def place_of(weights):
    rows = jnp.broadcast_to(weights, (16, weights.shape[1]))
    return places_of(rows)[:1]


def pick_kernel(capacity, tokens, me, both, *rest):
    out, place_out = rest[-2:]
    place = place_of(
        route_row(both, 2 * tokens, both.shape[0] - 2 * tokens, tokens, me[0] ^ 1)
    )
    place_out[...] = place
    pick = pick_of(place, capacity).astype(BF)
    out[:capacity] = dot(pick, both[:tokens]).astype(BF)
    out[capacity : 2 * capacity] = dot(pick, both[tokens : 2 * tokens]).astype(BF)
    out[2 * capacity :] = both[2 * tokens :]


def picked_rows(me, both, tokens, capacity, after=()):
    table = both.shape[0] - 2 * tokens
    return pl.pallas_call(
        functools.partial(pick_kernel, capacity, tokens),
        out_shape=[
            jax.ShapeDtypeStruct((2 * capacity + table, both.shape[1]), BF),
            jax.ShapeDtypeStruct((1, tokens), F32),
        ],
        in_specs=[ON_CHIP_SCALARS, ON_CHIP] + [ANYWHERE] * len(after),
        out_specs=[ON_CHIP] * 2,
        compiler_params=params(),
        cost_estimate=SMALL,
        name="pick",
    )(me, both, *after)


def grads_kernel(capacity, tokens, side, me, block, block_far, gate, up, down, *rest):
    out = rest[-1]
    half, ff = block.shape[1], gate.shape[1]
    table = (block.shape[0] - 2 * tokens - 2 * capacity) // 2
    slots = 2 * tokens + table
    weights = route_row(block, 2 * tokens, table, tokens, me[0])
    same = lax.broadcasted_iota(jnp.int32, (tokens, tokens), 0) == lax.broadcasted_iota(
        jnp.int32, (tokens, tokens), 1
    )
    dense_weight = jnp.sum(jnp.where(same, weights, 0.0), axis=1, keepdims=True)
    weights = route_row(block, slots + 2 * capacity, table, tokens, me[0])
    slot_weight = jnp.sum(
        pick_of(place_of(weights), capacity) * weights, axis=1, keepdims=True
    )
    weight = jnp.concatenate([dense_weight, slot_weight], axis=0)
    near = pl.ds(pl.multiple_of(side[0] * half, 256), half)
    far = pl.ds(pl.multiple_of((1 - side[0]) * half, 256), half)

    def feats(block):
        return jnp.concatenate([block[:tokens], block[slots : slots + capacity]], axis=0)

    def cots(block):
        second = slots + capacity
        return jnp.concatenate(
            [block[tokens : 2 * tokens], block[second : second + capacity]], axis=0
        )

    width = ff // 2
    for at in range(0, ff, width):
        cols = slice(at, at + width)
        rows, rows_far = feats(block), feats(block_far)
        gate_pre = dot(rows, gate[near, cols]) + dot(rows_far, gate[far, cols])
        up_pre = dot(rows, up[near, cols]) + dot(rows_far, up[far, cols])
        rows, rows_far = cots(block), cots(block_far)
        hidden = dot_t(rows, down[cols, near]) + dot_t(rows_far, down[cols, far])
        hidden = hidden * weight
        sig = jax.nn.sigmoid(gate_pre)
        out[:, cols] = (hidden * up_pre * sig * (1.0 + gate_pre * (1.0 - sig))).astype(BF)
        out[:, ff + at : ff + at + width] = (hidden * gate_pre * sig).astype(BF)


def grads_of(side, me, block, mats, tokens, capacity, after=()):
    return pl.pallas_call(
        functools.partial(grads_kernel, capacity, tokens),
        out_shape=jax.ShapeDtypeStruct((tokens + capacity, 2 * mats[0].shape[1]), BF),
        in_specs=[ON_CHIP_SCALARS] * 2 + [ON_CHIP] * 5 + [ANYWHERE] * len(after),
        out_specs=ON_CHIP,
        compiler_params=params(),
        cost_estimate=SMALL,
        name="grads",
    )(side, me, *block, *mats, *after)


def keep_kernel(side, gate, up, out, sems):
    half = out.shape[1]
    near = pl.ds(pl.multiple_of(side[0] * half, 256), half)
    copies = [
        pltpu.make_async_copy(ref.at[near], out.at[i], sems.at[i])
        for i, ref in enumerate((gate, up))
    ]
    for copy in copies:
        copy.start()
    for copy in copies:
        copy.wait()


def kept(side, gate, up):
    rows, ff = gate.shape
    return pl.pallas_call(
        keep_kernel,
        out_shape=jax.ShapeDtypeStruct((2, rows // 2, ff), BF),
        in_specs=[ON_CHIP_SCALARS] + [ANYWHERE] * 2,
        out_specs=ON_CHIP,
        scratch_shapes=[pltpu.SemaphoreType.DMA((2,))],
        compiler_params=params(),
        cost_estimate=SMALL,
        name="keep",
    )(side, gate, up)


def back_kernel(side, own, other, gate, up, far, *rest):
    dense, slots = rest[-2:]
    tokens, half = dense.shape
    ff = gate.shape[1]
    width = 256
    for at in range(0, half, width):
        near, cols = pl.ds(pl.multiple_of(side[0] * half + at, 256), width), slice(at, at + width)
        total = dot_t(own[:, :ff], gate[near, :]) + dot_t(own[:, ff:], up[near, :])
        total += dot_t(other[:, :ff], far[0, cols]) + dot_t(other[:, ff:], far[1, cols])
        dense[:, cols] = total[:tokens]
        slots[:, cols] = total[tokens:].astype(BF)


def back_of(side, own, other, mats, mats_far, tokens, after=()):
    rows, half = own.shape[0], mats_far.shape[1]
    return pl.pallas_call(
        back_kernel,
        out_shape=[
            jax.ShapeDtypeStruct((tokens, half), F32),
            jax.ShapeDtypeStruct((rows - tokens, half), BF),
        ],
        in_specs=[ON_CHIP_SCALARS] + [ON_CHIP] * 5 + [ANYWHERE] * len(after),
        out_specs=[ON_CHIP] * 2,
        compiler_params=params(),
        cost_estimate=SMALL,
        name="back",
    )(side, own, other, *mats, mats_far, *after)


def spread(place, came):
    pick = pick_of(place, came.shape[0]).astype(BF)
    return lax.dot_general(pick, came, (((0,), (0,)), ((), ())), preferred_element_type=F32)


def join_kernel(parts, place, came, dense, *rest):
    out = rest[-1]
    total = dense[...] + spread(place[...], came[...])
    for part in rest[:parts]:
        total = total + part[...].astype(F32)
    out[...] = total.astype(out.dtype)


def joined(place, came, dense, parts=(), dtype=BF, after=()):
    return pl.pallas_call(
        functools.partial(join_kernel, len(parts)),
        out_shape=jax.ShapeDtypeStruct(dense.shape, dtype),
        in_specs=[pl.BlockSpec(memory_space=pltpu.VMEM)] * (3 + len(parts))
        + [ANYWHERE] * len(after),
        out_specs=pl.BlockSpec(memory_space=pltpu.VMEM),
        compiler_params=params(),
        cost_estimate=SMALL,
        name="join",
    )(place, came, dense, *parts, *after)


def lines(tokens, out_grad, route_weight, expert_ids, w_gate, w_up, w_down):
    tok_rows, half = tokens.shape
    experts = lax.axis_size("node")
    top_count = expert_ids.shape[1]
    capacity = 3 * tok_rows * top_count // (2 * experts)
    me = lax.axis_index("node").astype(jnp.int32)
    z, me1 = me // 2, me[None]
    side = lax.axis_index("local").astype(jnp.int32)
    side1 = side[None]
    gate, up, down = w_gate[0], w_up[0], w_down[0]

    def late(value, *before):
        return lax.optimization_barrier((value, *before))[0]

    def halves(block):
        return block, swap(block)

    def rows_across(block, after=()):
        return picked_rows(me1, block, tok_rows, capacity, after)

    def grads(block, after=()):
        return grads_of(side1, me1, block, (gate, up, down), tok_rows, capacity, after)

    def joint(block, slots):
        return halves(jnp.concatenate([block, slots], axis=0))

    table = jnp.sum(
        jnp.where(
            expert_ids[None] == jnp.arange(experts, dtype=jnp.int32)[:, None, None],
            route_weight[None],
            0.0,
        ),
        axis=2,
    )
    both = stacked(tokens, out_grad, table)
    b_up, b_down = move(both, UP1), move(both, DOWN1)
    own_rows, place0 = rows_across(both)
    own_y = move(own_rows, Y_ALL)
    gate_far, up_far = swap(gate), swap(up)

    def back(own, after=()):
        return back_of(side1, *own, (gate, up), far_mats, tok_rows, after)

    b_up, b_down, own_y, gate_far, up_far = lax.optimization_barrier(
        (b_up, b_down, own_y, gate_far, up_far)
    )
    far_mats = kept(side1, gate_far, up_far)
    up_two, down_two = move(b_up, UP2), move(b_down, DOWN2)
    up_rows, place1 = rows_across(b_up)
    up_y = move(up_rows, Y_UP)
    grads0 = grads(joint(both, own_y), (up_rows, far_mats))

    up_two, down_two, grads0, up_y = lax.optimization_barrier((up_two, down_two, grads0, up_y))
    b_two = jnp.where(z >= 2, up_two, down_two)
    b_far = move(b_two, ENDS)
    down_rows, place2 = rows_across(b_down, (b_two,))
    down_y = move(down_rows, Y_DOWN)
    two_rows, place3 = rows_across(b_two, (down_rows,))
    two_y = move(two_rows, Y_ALL)
    dense0, slots0 = back(halves(grads0), (two_rows,))
    grads1 = grads(joint(b_up, up_y), (dense0,))

    b_far, slots0, grads1, two_y = lax.optimization_barrier((b_far, slots0, grads1, two_y))
    far_rows, place4 = rows_across(b_far)
    far_y = move(far_rows, Y_ENDS)
    dense1, slots1 = back(halves(late(grads1, far_rows)))
    grads3 = grads(joint(b_two, late(two_y, far_rows)), (dense1,))
    grads2 = grads(joint(b_down, late(down_y, far_rows)), (grads3,))

    came1 = move(slots1, Y_UP)
    join1 = joined(place1, came1, dense1, after=(grads2,))

    far_y, join1, grads2 = lax.optimization_barrier((far_y, join1, grads2))
    home1 = move(join1, DOWN1)
    dense3, slots3 = back(halves(late(grads3, far_y)))
    came3 = move(slots3, Y_ALL)
    grads4 = grads(joint(b_far, far_y), (dense3,))
    dense2, slots2 = back(halves(grads2), (grads4,))
    came2 = move(slots2, Y_DOWN)
    dense4, slots4 = back(halves(grads4), (dense2, home1))
    came4 = move(slots4, Y_ENDS)
    join3 = joined(place3, came3, dense3, after=(dense4,))
    home3 = move(join3, SKIP)
    join2 = joined(place2, came2, dense2, after=(join3,))
    home2 = move(join2, UP1)
    home4 = move(joined(place4, came4, dense4, after=(join2,)), FAR)
    came0 = move(late(slots0, dense4), Y_ALL)
    join0 = joined(place0, came0, dense0, (out_grad, home1), F32, (join2,))
    summed = join0
    for value in (home2, home3, home4):
        summed = summed + value.astype(F32)
    return summed.astype(BF)


def solution(mesh):
    placed = (
        P(("groups", "node"), "local"),
        P(("groups", "node"), "local"),
        P(("groups", "node"), None),
        P(("groups", "node"), None),
        P("node", None, "local"),
        P("node", None, "local"),
        P("node", "local", None),
    )
    body = lines if mesh.shape["node"] == 8 else exchanged
    return jax.shard_map(
        body, mesh=mesh, in_specs=placed, out_specs=P(("groups", "node"), "local"), check_vma=False
    )
```

```python
import functools

import jax
import jax.numpy as jnp
from jax import lax
from jax.experimental import pallas as pl
from jax.experimental.pallas import tpu as pltpu
from jax.sharding import PartitionSpec as P


def expert_grad(feat_rows, cot_rows, gate_mat, up_mat, down_mat):
    numbers = (((1,), (1,)), ((), ()))
    gate_pre = jnp.dot(feat_rows, gate_mat, preferred_element_type=jnp.float32)
    up_pre = jnp.dot(feat_rows, up_mat, preferred_element_type=jnp.float32)
    hidden_grad = lax.dot_general(cot_rows, down_mat, numbers, preferred_element_type=jnp.float32)
    gate_sig = jax.nn.sigmoid(gate_pre)
    gate_grad = (hidden_grad * up_pre * gate_sig * (1.0 + gate_pre * (1.0 - gate_sig))).astype(
        jnp.bfloat16
    )
    up_grad = (hidden_grad * gate_pre * gate_sig).astype(jnp.bfloat16)
    summed = lax.dot_general(gate_grad, gate_mat, numbers, preferred_element_type=jnp.float32)
    return summed + lax.dot_general(up_grad, up_mat, numbers, preferred_element_type=jnp.float32)


def exchanged(tokens, out_grad, route_weight, expert_ids, w_gate, w_up, w_down):
    tok_rows, half_width = tokens.shape
    top_count = expert_ids.shape[1]
    experts = lax.axis_size("node")
    capacity = 3 * tok_rows * top_count // (2 * experts)
    flat_ids = expert_ids.reshape(-1)
    onehot = (flat_ids[:, None] == jnp.arange(experts, dtype=jnp.int32)[None, :]).astype(jnp.int32)
    earlier = jnp.cumsum(onehot, axis=0) - onehot
    slot_index = jnp.sum(earlier * onehot, axis=1)
    target = flat_ids * capacity + slot_index
    scaled = (
        route_weight.reshape(-1)[:, None]
        * jnp.repeat(out_grad, top_count, axis=0).astype(jnp.float32)
    ).astype(jnp.bfloat16)
    copies = jnp.repeat(tokens, top_count, axis=0)
    feat_send = jnp.zeros((experts * capacity, half_width), jnp.bfloat16).at[target].set(copies)
    cot_send = jnp.zeros((experts * capacity, half_width), jnp.bfloat16).at[target].set(scaled)
    feat_send = feat_send.reshape(experts, capacity, half_width)
    cot_send = cot_send.reshape(experts, capacity, half_width)

    def to_experts(sent):
        moved = lax.all_to_all(sent, "node", split_axis=0, concat_axis=0, tiled=True)
        return lax.all_gather(moved, "local", axis=2, tiled=True)

    feat_full = to_experts(feat_send)
    cot_full = to_experts(cot_send)
    sources, slot_count, feat_width = feat_full.shape
    partial_value = expert_grad(
        feat_full.reshape(-1, feat_width),
        cot_full.reshape(-1, feat_width),
        w_gate[0],
        w_up[0],
        w_down[0],
    )
    own_sum = lax.psum_scatter(
        partial_value.reshape(sources, slot_count, feat_width),
        "local",
        scatter_dimension=2,
        tiled=True,
    )
    returned = lax.all_to_all(
        own_sum.astype(jnp.bfloat16), "node", split_axis=0, concat_axis=0, tiled=True
    )
    picked = returned.reshape(experts * capacity, half_width)[target]
    summed = out_grad.astype(jnp.float32) + jnp.sum(
        picked.reshape(tok_rows, top_count, half_width).astype(jnp.float32), axis=1
    )
    return summed.astype(jnp.bfloat16)


def node(z, y):
    return 2 * z + y


def along(pairs):
    return [(node(a, y), node(b, y)) for a, b in pairs for y in range(2)]


def across(places):
    return [(node(z, y), node(z, 1 - y)) for z in places for y in range(2)]


UP1 = along([(0, 1), (1, 2), (2, 3)])
DOWN1 = along([(1, 0), (2, 1), (3, 2)])
UP2 = along([(1, 2), (2, 3)])
DOWN2 = along([(2, 1), (1, 0)])
ENDS = along([(2, 3), (1, 0)])
SKIP = along([(0, 2), (1, 3), (2, 0), (3, 1)])
FAR = along([(0, 3), (3, 0)])
Y_ALL, Y_UP, Y_DOWN, Y_ENDS = across(range(4)), across([1, 2, 3]), across([0, 1, 2]), across([0, 3])
SLOTS = 5
BF, F32 = jnp.bfloat16, jnp.float32
ON_CHIP = pl.BlockSpec(memory_space=pltpu.VMEM)
ON_CHIP_SCALARS = pl.BlockSpec(memory_space=pltpu.SMEM)
ANYWHERE = pl.BlockSpec(memory_space=pl.ANY)
SMALL = pl.CostEstimate(flops=1024, bytes_accessed=1024, transcendentals=0)


def move(value, pairs):
    return lax.ppermute(value, "node", pairs)


def swap(value):
    return lax.ppermute(value, "local", [(0, 1), (1, 0)])


def dot(a, b):
    return jnp.dot(a, b, preferred_element_type=F32)


def dot_t(a, b):
    return lax.dot_general(a, b, (((1,), (1,)), ((), ())), preferred_element_type=F32)


def params():
    return pltpu.CompilerParams(vmem_limit_bytes=16 * 1024 * 1024)


def places_of(weights):
    tokens = weights.shape[-1]
    earlier = lax.broadcasted_iota(jnp.int32, (tokens, tokens), 0) < lax.broadcasted_iota(
        jnp.int32, (tokens, tokens), 1
    )
    routed = (weights > 0.0).astype(F32)
    place = dot(routed.astype(BF), earlier.astype(F32).astype(BF))
    return jnp.where(weights > 0.0, place, -1.0)


def pick_of(place, capacity):
    slots = lax.broadcasted_iota(jnp.int32, (capacity, place.shape[-1]), 0).astype(F32)
    return jnp.where(slots == place, 1.0, 0.0).astype(F32)


def stack_kernel(feat, cot, table, out):
    tokens, half = feat.shape
    out[:tokens] = feat[...]
    out[tokens : 2 * tokens] = cot[...]
    value = table[...]
    high = value.astype(BF).astype(F32)
    middle = (value - high).astype(BF).astype(F32)
    low = value - high - middle
    upper = jnp.concatenate([high, low], axis=1)
    lower = jnp.concatenate([middle, jnp.zeros_like(low)], axis=1)
    rows = jnp.concatenate([upper, lower], axis=0)
    rest = jnp.zeros((rows.shape[0], half - rows.shape[1]), F32)
    out[2 * tokens :] = jnp.concatenate([rows, rest], axis=1).astype(BF)


def stacked(feat, cot, table):
    tokens, half = feat.shape
    return pl.pallas_call(
        stack_kernel,
        out_shape=jax.ShapeDtypeStruct((2 * tokens + 2 * table.shape[0], half), BF),
        in_specs=[ON_CHIP] * 3,
        out_specs=ON_CHIP,
        compiler_params=params(),
        cost_estimate=SMALL,
        name="stack",
    )(feat, cot, table)


def route_row(ref, first, height, tokens, expert):
    rows = ref[first : first + height, : 2 * tokens].astype(F32)
    count = rows.shape[0] // 2
    table = rows[:count, :tokens] + rows[count:, :tokens] + rows[:count, tokens:]
    chosen = lax.broadcasted_iota(jnp.int32, table.shape, 0) == expert
    return jnp.sum(jnp.where(chosen, table, 0.0), axis=0, keepdims=True)


def place_of(weights):
    rows = jnp.broadcast_to(weights, (16, weights.shape[1]))
    return places_of(rows)[:1]


def pick_kernel(capacity, tokens, me, both, *rest):
    out, place_out = rest[-2:]
    place = place_of(
        route_row(both, 2 * tokens, both.shape[0] - 2 * tokens, tokens, me[0] ^ 1)
    )
    place_out[...] = place
    pick = pick_of(place, capacity).astype(BF)
    out[:capacity] = dot(pick, both[:tokens]).astype(BF)
    out[capacity : 2 * capacity] = dot(pick, both[tokens : 2 * tokens]).astype(BF)
    out[2 * capacity :] = both[2 * tokens :]


def picked_rows(me, both, tokens, capacity, after=()):
    table = both.shape[0] - 2 * tokens
    return pl.pallas_call(
        functools.partial(pick_kernel, capacity, tokens),
        out_shape=[
            jax.ShapeDtypeStruct((2 * capacity + table, both.shape[1]), BF),
            jax.ShapeDtypeStruct((1, tokens), F32),
        ],
        in_specs=[ON_CHIP_SCALARS, ON_CHIP] + [ANYWHERE] * len(after),
        out_specs=[ON_CHIP] * 2,
        compiler_params=params(),
        cost_estimate=SMALL,
        name="pick",
    )(me, both, *after)


def grads_kernel(capacity, tokens, side, me, block, block_far, gate, up, down, *rest):
    out = rest[-1]
    half, ff = block.shape[1], gate.shape[1]
    table = (block.shape[0] - 2 * tokens - 2 * capacity) // 2
    slots = 2 * tokens + table
    weights = route_row(block, 2 * tokens, table, tokens, me[0])
    same = lax.broadcasted_iota(jnp.int32, (tokens, tokens), 0) == lax.broadcasted_iota(
        jnp.int32, (tokens, tokens), 1
    )
    dense_weight = jnp.sum(jnp.where(same, weights, 0.0), axis=1, keepdims=True)
    weights = route_row(block, slots + 2 * capacity, table, tokens, me[0])
    slot_weight = jnp.sum(
        pick_of(place_of(weights), capacity) * weights, axis=1, keepdims=True
    )
    weight = jnp.concatenate([dense_weight, slot_weight], axis=0)
    near = pl.ds(pl.multiple_of(side[0] * half, 256), half)
    far = pl.ds(pl.multiple_of((1 - side[0]) * half, 256), half)

    def feats(block):
        return jnp.concatenate([block[:tokens], block[slots : slots + capacity]], axis=0)

    def cots(block):
        second = slots + capacity
        return jnp.concatenate(
            [block[tokens : 2 * tokens], block[second : second + capacity]], axis=0
        )

    width = ff // 2
    for at in range(0, ff, width):
        cols = slice(at, at + width)
        rows, rows_far = feats(block), feats(block_far)
        gate_pre = dot(rows, gate[near, cols]) + dot(rows_far, gate[far, cols])
        up_pre = dot(rows, up[near, cols]) + dot(rows_far, up[far, cols])
        rows, rows_far = cots(block), cots(block_far)
        hidden = dot_t(rows, down[cols, near]) + dot_t(rows_far, down[cols, far])
        hidden = hidden * weight
        sig = jax.nn.sigmoid(gate_pre)
        out[:, cols] = (hidden * up_pre * sig * (1.0 + gate_pre * (1.0 - sig))).astype(BF)
        out[:, ff + at : ff + at + width] = (hidden * gate_pre * sig).astype(BF)


def grads_of(side, me, block, mats, tokens, capacity, after=()):
    return pl.pallas_call(
        functools.partial(grads_kernel, capacity, tokens),
        out_shape=jax.ShapeDtypeStruct((tokens + capacity, 2 * mats[0].shape[1]), BF),
        in_specs=[ON_CHIP_SCALARS] * 2 + [ON_CHIP] * 5 + [ANYWHERE] * len(after),
        out_specs=ON_CHIP,
        compiler_params=params(),
        cost_estimate=SMALL,
        name="grads",
    )(side, me, *block, *mats, *after)


def keep_kernel(side, gate, up, out, sems):
    half = out.shape[1]
    near = pl.ds(pl.multiple_of(side[0] * half, 256), half)
    copies = [
        pltpu.make_async_copy(ref.at[near], out.at[i], sems.at[i])
        for i, ref in enumerate((gate, up))
    ]
    for copy in copies:
        copy.start()
    for copy in copies:
        copy.wait()


def kept(side, gate, up):
    rows, ff = gate.shape
    return pl.pallas_call(
        keep_kernel,
        out_shape=jax.ShapeDtypeStruct((2, rows // 2, ff), BF),
        in_specs=[ON_CHIP_SCALARS] + [ANYWHERE] * 2,
        out_specs=ON_CHIP,
        scratch_shapes=[pltpu.SemaphoreType.DMA((2,))],
        compiler_params=params(),
        cost_estimate=SMALL,
        name="keep",
    )(side, gate, up)


def back_kernel(side, own, other, gate, up, far, *rest):
    dense, slots = rest[-2:]
    tokens, half = dense.shape
    ff = gate.shape[1]
    width = 256
    for at in range(0, half, width):
        near, cols = pl.ds(pl.multiple_of(side[0] * half + at, 256), width), slice(at, at + width)
        total = dot_t(own[:, :ff], gate[near, :]) + dot_t(own[:, ff:], up[near, :])
        total += dot_t(other[:, :ff], far[0, cols]) + dot_t(other[:, ff:], far[1, cols])
        dense[:, cols] = total[:tokens]
        slots[:, cols] = total[tokens:].astype(BF)


def back_of(side, own, other, mats, mats_far, tokens, after=()):
    rows, half = own.shape[0], mats_far.shape[1]
    return pl.pallas_call(
        back_kernel,
        out_shape=[
            jax.ShapeDtypeStruct((tokens, half), F32),
            jax.ShapeDtypeStruct((rows - tokens, half), BF),
        ],
        in_specs=[ON_CHIP_SCALARS] + [ON_CHIP] * 5 + [ANYWHERE] * len(after),
        out_specs=[ON_CHIP] * 2,
        compiler_params=params(),
        cost_estimate=SMALL,
        name="back",
    )(side, own, other, *mats, mats_far, *after)


def spread(place, came):
    pick = pick_of(place, came.shape[0]).astype(BF)
    return lax.dot_general(pick, came, (((0,), (0,)), ((), ())), preferred_element_type=F32)


def join_kernel(parts, place, came, dense, *rest):
    out = rest[-1]
    total = dense[...] + spread(place[...], came[...])
    for part in rest[:parts]:
        total = total + part[...].astype(F32)
    out[...] = total.astype(out.dtype)


def joined(place, came, dense, parts=(), dtype=BF, after=()):
    return pl.pallas_call(
        functools.partial(join_kernel, len(parts)),
        out_shape=jax.ShapeDtypeStruct(dense.shape, dtype),
        in_specs=[pl.BlockSpec(memory_space=pltpu.VMEM)] * (3 + len(parts))
        + [ANYWHERE] * len(after),
        out_specs=pl.BlockSpec(memory_space=pltpu.VMEM),
        compiler_params=params(),
        cost_estimate=SMALL,
        name="join",
    )(place, came, dense, *parts, *after)


def lines(tokens, out_grad, route_weight, expert_ids, w_gate, w_up, w_down):
    tok_rows, half = tokens.shape
    experts = lax.axis_size("node")
    top_count = expert_ids.shape[1]
    capacity = 3 * tok_rows * top_count // (2 * experts)
    me = lax.axis_index("node").astype(jnp.int32)
    z, me1 = me // 2, me[None]
    side = lax.axis_index("local").astype(jnp.int32)
    side1 = side[None]
    gate, up, down = w_gate[0], w_up[0], w_down[0]

    def late(value, *before):
        return lax.optimization_barrier((value, *before))[0]

    def halves(block):
        return block, swap(block)

    def rows_across(block, after=()):
        return picked_rows(me1, block, tok_rows, capacity, after)

    def grads(block, after=()):
        return grads_of(side1, me1, block, (gate, up, down), tok_rows, capacity, after)

    def joint(block, slots):
        return halves(jnp.concatenate([block, slots], axis=0))

    table = jnp.sum(
        jnp.where(
            expert_ids[None] == jnp.arange(experts, dtype=jnp.int32)[:, None, None],
            route_weight[None],
            0.0,
        ),
        axis=2,
    )
    both = stacked(tokens, out_grad, table)
    b_up, b_down = move(both, UP1), move(both, DOWN1)
    own_rows, place0 = rows_across(both)
    own_y = move(own_rows, Y_ALL)
    gate_far, up_far = swap(gate), swap(up)

    def back(own, after=()):
        return back_of(side1, *own, (gate, up), far_mats, tok_rows, after)

    b_up, b_down, own_y, gate_far, up_far = lax.optimization_barrier(
        (b_up, b_down, own_y, gate_far, up_far)
    )
    far_mats = kept(side1, gate_far, up_far)
    up_two, down_two = move(b_up, UP2), move(b_down, DOWN2)
    up_rows, place1 = rows_across(b_up)
    up_y = move(up_rows, Y_UP)
    grads0 = grads(joint(both, own_y), (up_rows, far_mats))

    up_two, down_two, grads0, up_y = lax.optimization_barrier((up_two, down_two, grads0, up_y))
    b_two = jnp.where(z >= 2, up_two, down_two)
    b_far = move(b_two, ENDS)
    down_rows, place2 = rows_across(b_down, (b_two,))
    down_y = move(down_rows, Y_DOWN)
    two_rows, place3 = rows_across(b_two, (down_rows,))
    two_y = move(two_rows, Y_ALL)
    dense0, slots0 = back(halves(grads0), (two_rows,))
    grads1 = grads(joint(b_up, up_y), (dense0,))

    b_far, slots0, grads1, two_y = lax.optimization_barrier((b_far, slots0, grads1, two_y))
    far_rows, place4 = rows_across(b_far)
    far_y = move(far_rows, Y_ENDS)
    dense1, slots1 = back(halves(late(grads1, far_rows)))
    grads3 = grads(joint(b_two, late(two_y, far_rows)), (dense1,))
    grads2 = grads(joint(b_down, late(down_y, far_rows)), (grads3,))

    came1 = move(slots1, Y_UP)
    join1 = joined(place1, came1, dense1, after=(grads2,))

    far_y, join1, grads2 = lax.optimization_barrier((far_y, join1, grads2))
    home1 = move(join1, DOWN1)
    dense3, slots3 = back(halves(late(grads3, far_y)))
    came3 = move(slots3, Y_ALL)
    grads4 = grads(joint(b_far, far_y), (dense3,))
    dense2, slots2 = back(halves(grads2), (grads4,))
    came2 = move(slots2, Y_DOWN)
    dense4, slots4 = back(halves(grads4), (dense2, home1))
    came4 = move(slots4, Y_ENDS)
    join3 = joined(place3, came3, dense3, after=(dense2,))
    home3 = move(join3, SKIP)
    join2 = joined(place2, came2, dense2, after=(join3,))
    home2 = move(join2, UP1)
    home4 = move(joined(place4, came4, dense4, after=(join2,)), FAR)
    came0 = move(late(slots0, dense4), Y_ALL)
    join0 = joined(place0, came0, dense0, (out_grad, home1), F32, (join2,))
    summed = join0
    for value in (home2, home3, home4):
        summed = summed + value.astype(F32)
    return summed.astype(BF)


def solution(mesh):
    placed = (
        P(("groups", "node"), "local"),
        P(("groups", "node"), "local"),
        P(("groups", "node"), None),
        P(("groups", "node"), None),
        P("node", None, "local"),
        P("node", None, "local"),
        P("node", "local", None),
    )
    body = lines if mesh.shape["node"] == 8 else exchanged
    return jax.shard_map(
        body, mesh=mesh, in_specs=placed, out_specs=P(("groups", "node"), "local"), check_vma=False
    )
```
